32 devices in a mesh: groups: 2 (over y), wide: 16 (over z, x, core).
Axes of the slice: x: 2, y: 2, z: 4, core: 2. Of those that a mesh axis runs over, the one named last changes fastest.
Arguments:
- points: float32 [64, 393216], P(None, ('groups', 'wide')), parts along dimension 1
- solution: float32 [32, 393216], P(None, ('groups', 'wide')), parts along dimension 1, may hold values from -6 to 6
- residual: float32 [32, 393216], P(None, ('groups', 'wide')), parts along dimension 1, may hold values from -6 to 6
- direction: float32 [32, 393216], P(None, ('groups', 'wide')), parts along dimension 1, may hold values from -6 to 6
- lengthscales: float32 [4], replicated, may hold values from 0.5 to 1
- noise_variance: float32 [4], replicated, may hold values from 0.1 to 1
- link_peer: int32 [32, 48, 2], P(('groups', 'wide')), parts along dimension 0, may hold values from 0 to 15, as said below
Outputs:
- new_solution: float32 [32, 393216], P(None, ('groups', 'wide')), parts along dimension 1
- new_residual: float32 [32, 393216], P(None, ('groups', 'wide')), parts along dimension 1
- new_direction: float32 [32, 393216], P(None, ('groups', 'wide')), parts along dimension 1
The draws below stay inside these ranges and needn't reach their ends.
There are 2 independent parts, one for each index of `groups`. The reference program is written for one: setup_inputs(seed, part) draws one part's arguments, and reference() takes and returns one part's arrays. A program takes and returns all parts, laid end to end along the dimension named above; an argument that names none is the same for every part. Nothing has to cross between parts.
Inputs may be any that keep to these rules, and one draw needn't show every extreme that they name: `link_peer`: local block t of a device is linked with local block t of two other devices, named on side 0 and side 1: in a cyclic order of the devices drawn with the seed, they stand k places before and k places after it, with k = 1 + (t mod 7). What a device names on side 1 names it on side 0 for the same t. A device is linked with a given peer only through blocks t of one residue of t mod 7, hence through at most 7 blocks, and some pair of devices is linked through 7 blocks.
All inputs are finite; a program needn't handle non-finite values.
Results may differ from the reference program's by a relative error of at most 0.0003.
Values sent between devices are 32-bit elements; how exact they have to be, the bound alone decides.
A program may use at most 128 MiB of HBM per device.

```python
import math
import jax
import jax.numpy as jnp
from jax import lax

FEATURES = 64
SETTINGS = 4
PROBES = 8
BLOCK_POINTS = 256
BLOCKS = 48
COLUMNS = 32
POINTS = 196608
ROUNDS = 7
N_WIDE = 16


def layout(key):
    device_order = jax.random.permutation(jax.random.fold_in(key, 101), N_WIDE).astype(jnp.int32)
    place = jnp.zeros((N_WIDE,), jnp.int32).at[device_order].set(jnp.arange(N_WIDE, dtype=jnp.int32))
    return (device_order, place)


def neighbours(device_order, place, round_index):
    stride = 1 + round_index % ROUNDS
    left_peer = device_order[(place - stride) % N_WIDE]
    right_peer = device_order[(place + stride) % N_WIDE]
    return (left_peer, right_peer)


def draw_link_peer(key, part):
    device_order, place = layout(key)
    sides = []
    for round_index in range(BLOCKS):
        left_peer, right_peer = neighbours(device_order, place, round_index)
        sides.append(jnp.stack([left_peer, right_peer], axis=1))
    return jnp.stack(sides, axis=1).astype(jnp.int32)


def draw_points(key, part):
    device_order, place = layout(key)
    key = jax.random.fold_in(key, 7)
    first_axis = jnp.zeros((FEATURES,), jnp.float32).at[0].set(1.0)
    second_axis = jnp.zeros((FEATURES,), jnp.float32).at[1].set(1.0)
    per_round = []
    for round_index in range(BLOCKS):
        stride = 1 + round_index % ROUNDS
        common = math.gcd(N_WIDE, stride)
        cycle_length = N_WIDE // common
        inverse = pow(stride // common, -1, cycle_length)
        cycle_index = place % common
        arc_index = (place - cycle_index) // common * inverse % cycle_length
        radius = cycle_length * 0.04 / (2.0 * math.pi)
        spread = jax.random.uniform(jax.random.fold_in(key, 2 * round_index), (N_WIDE, BLOCK_POINTS), jnp.float32)
        angle = 2.0 * math.pi * (arc_index[:, None].astype(jnp.float32) + spread) / cycle_length
        first_coord = radius * jnp.cos(angle) + cycle_index[:, None].astype(jnp.float32) * (2.0 * radius + 4.0)
        second_coord = radius * jnp.sin(angle)
        jitter = 0.002 * jax.random.normal(jax.random.fold_in(key, 2 * round_index + 1), (N_WIDE, BLOCK_POINTS, FEATURES), jnp.float32)
        marker = jnp.zeros((FEATURES,), jnp.float32).at[2 + round_index].set(2.0)
        block_values = jitter + marker + first_coord[:, :, None] * first_axis + second_coord[:, :, None] * second_axis
        per_round.append(block_values)
    stacked = jnp.stack(per_round, axis=1)
    return jnp.transpose(stacked, (3, 0, 1, 2)).reshape(FEATURES, N_WIDE * BLOCKS * BLOCK_POINTS).astype(jnp.float32)


def block_levels(rng, shape, cuts, smallest, largest):
    gain, own = 1.0, jax.random.fold_in(rng, 6)
    for axis_at, parts in cuts:
        draws = jnp.exp(jax.random.uniform(jax.random.fold_in(own, axis_at), (parts,), jnp.float32, smallest / len(cuts), largest / len(cuts)))
        gain = gain * jnp.repeat(draws, shape[axis_at] // parts).reshape([-1 if axis == axis_at else 1 for axis in range(len(shape))])
    return gain


def noise(key, dims, scale, bound, shards=(), kind=jnp.bfloat16):
    values = scale * jax.random.normal(key, dims, jnp.float32)
    if shards:
        values = values * block_levels(key, dims, shards, -0.22, 0.18)
    return jnp.clip(values, -bound, bound).astype(kind)


def setup_inputs(seed: int = 0, part: int = 0) -> dict:
    splits = jax.random.split(jax.random.key(seed), 8)
    part_keys = jax.random.split(jax.random.fold_in(splits[7], part), 8)
    points = draw_points(jax.random.fold_in(jax.random.fold_in(splits[7], part), 71), part)
    solution = noise(part_keys[1], (COLUMNS, POINTS), 1.0, 6.0, ((1, 16),), jnp.float32)
    residual = noise(part_keys[2], (COLUMNS, POINTS), 1.0, 6.0, ((1, 16),), jnp.float32)
    direction = noise(part_keys[3], (COLUMNS, POINTS), 1.0, 6.0, ((1, 16),), jnp.float32)
    lengthscales = jnp.clip(jnp.exp(jax.random.uniform(splits[4], (SETTINGS,), jnp.float32, math.log(0.5), math.log(1.0))), 0.5, 1.0)
    noise_variance = jnp.clip(jnp.exp(jax.random.uniform(splits[5], (SETTINGS,), jnp.float32, math.log(0.1), math.log(1.0))), 0.1, 1.0)
    link_peer = draw_link_peer(jax.random.fold_in(jax.random.fold_in(splits[7], part), 71), part)
    return dict(points=points, solution=solution, residual=residual, direction=direction, lengthscales=lengthscales, noise_variance=noise_variance, link_peer=link_peer)


highest = lax.Precision.HIGHEST

def kernel_tile(row_points, col_points, lengthscales):
    anchor = row_points[:, :, :1]
    row_shift = row_points - anchor
    col_shift = col_points - anchor
    row_norms = lax.optimization_barrier(jnp.sum(row_shift * row_shift, axis=1))
    col_norms = lax.optimization_barrier(jnp.sum(col_shift * col_shift, axis=1))
    inner_product = jnp.einsum('gda,gdb->gab', row_shift, col_shift, precision=highest)
    squared = row_norms[:, :, None] + col_norms[:, None, :] - 2.0 * inner_product
    distance = jnp.sqrt(jnp.maximum(squared, 0.0))
    scaled = distance[:, None, :, :] / lengthscales[None, :, None, None]
    support = jnp.maximum(1.0 - scaled, 0.0)
    return support ** 35 * (35.0 * scaled + 1.0)

def apply_ahead(kernel, vectors):
    return jnp.einsum('gsab,gsrb->gsra', kernel, vectors, precision=highest)

def apply_behind(kernel, vectors):
    return jnp.einsum('gsab,gsra->gsrb', kernel, vectors, precision=highest)

def reference(points, solution, residual, direction, lengthscales, noise_variance, link_peer):
    block_coords = jnp.transpose(points.reshape(FEATURES, N_WIDE, BLOCKS, BLOCK_POINTS), (1, 2, 0, 3))
    block_vectors = jnp.transpose(direction.reshape(SETTINGS, PROBES, N_WIDE, BLOCKS, BLOCK_POINTS), (2, 3, 0, 1, 4))
    devices = jnp.broadcast_to(jnp.arange(N_WIDE, dtype=jnp.int32)[:, None], (N_WIDE, BLOCKS))
    rounds = jnp.broadcast_to(jnp.arange(BLOCKS, dtype=jnp.int32)[None, :], (N_WIDE, BLOCKS))
    neighbour = link_peer[:, :, 1]
    owns_right = devices < neighbour
    owner_device = jnp.where(owns_right, devices, neighbour).astype(jnp.int32)
    other_device = jnp.where(owns_right, neighbour, devices).astype(jnp.int32)

    def pair_terms(group_items):
        owner_index, other_index, round_index = group_items
        owner_points = block_coords[owner_index, round_index]
        other_points = block_coords[other_index, round_index]
        kernel = kernel_tile(owner_points, other_points, lengthscales)
        ahead = apply_ahead(kernel, block_vectors[other_index, round_index])
        behind = apply_behind(kernel, block_vectors[owner_index, round_index])
        return (ahead, behind)
    ahead, behind = lax.map(pair_terms, (owner_device.reshape(-1, 8), other_device.reshape(-1, 8), rounds.reshape(-1, 8)))

    def diagonal_terms(group_items):
        own_points, own_vectors = group_items
        return apply_ahead(kernel_tile(own_points, own_points, lengthscales), own_vectors)
    diagonal = lax.map(diagonal_terms, (block_coords.reshape(-1, 8, FEATURES, BLOCK_POINTS), block_vectors.reshape(-1, 8, SETTINGS, PROBES, BLOCK_POINTS)))
    product = diagonal.reshape(N_WIDE, BLOCKS, SETTINGS, PROBES, BLOCK_POINTS)
    product = product.at[owner_device.reshape(-1), rounds.reshape(-1)].add(ahead.reshape(-1, SETTINGS, PROBES, BLOCK_POINTS))
    product = product.at[other_device.reshape(-1), rounds.reshape(-1)].add(behind.reshape(-1, SETTINGS, PROBES, BLOCK_POINTS))
    product_flat = jnp.transpose(product, (2, 3, 0, 1, 4)).reshape(COLUMNS, POINTS)
    noise_columns = jnp.repeat(noise_variance, PROBES)[:, None]
    image_field = noise_columns * direction + product_flat
    old_norm = lax.optimization_barrier(jnp.sum(residual * residual, axis=1))
    curvature = lax.optimization_barrier(jnp.sum(direction * image_field, axis=1))
    step_size = (old_norm / curvature)[:, None]
    new_solution = solution + step_size * direction
    new_residual = residual - step_size * image_field
    new_norm = lax.optimization_barrier(jnp.sum(new_residual * new_residual, axis=1))
    new_direction = new_residual + (new_norm / old_norm)[:, None] * direction
    return (new_solution, new_residual, new_direction)
```

```python
import functools

import jax
import jax.numpy as jnp
from jax import lax
from jax.experimental import pallas as pl
from jax.experimental.pallas import tpu as pltpu
from jax.sharding import PartitionSpec as P

VMEM = pltpu.VMEM
SMEM = pltpu.SMEM
VMEM_LIMIT = 56 * 1024 * 1024
SCALE = 35.0 ** (1.0 / 36.0)
TOP = 36.0 * SCALE / 35.0
ROW_CHUNK = 32


def split_three(x):
    first = x.astype(jnp.bfloat16)
    rest = x - first.astype(jnp.float32)
    second = rest.astype(jnp.bfloat16)
    third = (rest - second.astype(jnp.float32)).astype(jnp.bfloat16)
    return first, second, third


def norm_rows(norms, low):
    pieces = [piece.astype(jnp.float32) for piece in split_three(norms)]
    row = lax.broadcasted_iota(jnp.int32, (16, norms.shape[1]), 0)
    rows = jnp.where((row >= 3 - low) & (row < 6 - low), 1.0, 0.0)
    for index, piece in enumerate(pieces):
        rows = jnp.where(row == index + low, piece, rows)
    return rows.astype(jnp.bfloat16)


def squared_distances(row_shift, col_shift):
    row_norms = jnp.sum(row_shift * row_shift, axis=0, keepdims=True)
    col_norms = jnp.sum(col_shift * col_shift, axis=0, keepdims=True)
    r1, r2, r3 = split_three(row_shift)
    c1, c2, c3 = split_three(-2.0 * col_shift)
    left = jnp.concatenate([r1, r1, r2, r1, r3, r2, norm_rows(row_norms, 0)], axis=0)
    right = jnp.concatenate([c1, c2, c1, c3, c1, c2, norm_rows(col_norms, 3)], axis=0)
    return lax.dot_general(
        left, right, (((0,), (0,)), ((), ())), preferred_element_type=jnp.float32
    )


def split_vectors(vectors, setting, probes):
    rows = vectors[setting * probes : (setting + 1) * probes]
    high = rows.astype(jnp.bfloat16).astype(jnp.float32)
    return jnp.concatenate([high, rows - high], axis=0).astype(jnp.bfloat16)


def apply_tile(vectors, high, low, dim):
    dims = (((1,), (dim,)), ((), ()))
    both = lax.dot_general(vectors, high, dims, preferred_element_type=jnp.float32)
    both += lax.dot_general(vectors, low, dims, preferred_element_type=jnp.float32)
    half = both.shape[0] // 2
    return both[:half] + both[half:]


def tile_products(inverse_ref, row_shift, col_shift, row_vectors, col_vectors, dist_ref, high_ref, low_ref, probes):
    size = row_shift.shape[1]
    settings = high_ref.shape[0]
    floor = jnp.maximum(squared_distances(row_shift, col_shift), 1e-30)
    dist_ref[...] = floor * lax.rsqrt(floor)
    ahead, behind = [], []
    for setting in range(settings):
        inverse = inverse_ref[setting]
        for start in range(0, size, ROW_CHUNK):
            rows = pl.ds(start, ROW_CHUNK)
            w = jnp.maximum(SCALE - dist_ref[rows, :] * inverse, 0.0)
            w2 = w * w
            w4 = w2 * w2
            w8 = w4 * w4
            w16 = w8 * w8
            w32 = w16 * w16
            value = (w32 * (w2 * w)) * (TOP - w)
            high = value.astype(jnp.bfloat16)
            high_ref[setting, rows, :] = high
            low_ref[setting, rows, :] = (value - high.astype(jnp.float32)).astype(jnp.bfloat16)
        high, low = high_ref[setting], low_ref[setting]
        behind.append(apply_tile(split_vectors(row_vectors, setting, probes), high, low, 0))
        if col_vectors is not None:
            ahead.append(apply_tile(split_vectors(col_vectors, setting, probes), high, low, 1))
    behind = jnp.concatenate(behind, axis=0)
    return (jnp.concatenate(ahead, axis=0) if ahead else None), behind


def gather_kernel(size, index_ref, points_ref, direction_ref, out_ref, sem):
    features = points_ref.shape[0]
    columns = direction_ref.shape[0]

    def start(item, carry):
        block = pl.ds(pl.multiple_of(index_ref[item] * size, size), size)
        pltpu.make_async_copy(points_ref.at[:, block], out_ref.at[item, pl.ds(0, features)], sem).start()
        pltpu.make_async_copy(direction_ref.at[:, block], out_ref.at[item, pl.ds(features, columns)], sem).start()
        return carry

    lax.fori_loop(0, out_ref.shape[0], start, 0)
    pltpu.make_async_copy(out_ref, out_ref, sem).wait()


def gather_blocks(index, points, direction, size):
    rows = points.shape[0] + direction.shape[0]
    return pl.pallas_call(
        functools.partial(gather_kernel, size),
        out_shape=jax.ShapeDtypeStruct((index.shape[0], rows, size), jnp.float32),
        in_specs=[pl.BlockSpec(memory_space=SMEM)] + [pl.BlockSpec(memory_space=pl.ANY)] * 2,
        out_specs=pl.BlockSpec(memory_space=pl.ANY),
        scratch_shapes=[pltpu.SemaphoreType.DMA],
    )(index, points, direction)


def diagonal_kernel(size, probes, inverse_ref, points_ref, direction_ref, out_ref, dist_ref, high_ref, low_ref):
    def turn(block, carry):
        at = pl.ds(pl.multiple_of(block * size, size), size)
        own = points_ref[:, at]
        shift = own - own[:, 0:1]
        _, product = tile_products(
            inverse_ref, shift, shift, direction_ref[:, at], None, dist_ref, high_ref, low_ref, probes
        )
        out_ref[:, at] = product
        return carry

    lax.fori_loop(0, points_ref.shape[1] // size, turn, 0)


def tile_scratch(settings, size):
    return [
        pltpu.VMEM((size, size), jnp.float32),
        pltpu.VMEM((settings, size, size), jnp.bfloat16),
        pltpu.VMEM((settings, size, size), jnp.bfloat16),
    ]


def diagonal_products(inverse, points, direction, size):
    settings = inverse.shape[0]
    return pl.pallas_call(
        functools.partial(diagonal_kernel, size, direction.shape[0] // settings),
        out_shape=jax.ShapeDtypeStruct(direction.shape, jnp.float32),
        in_specs=[pl.BlockSpec(memory_space=SMEM)] + [pl.BlockSpec(memory_space=VMEM)] * 2,
        out_specs=pl.BlockSpec(memory_space=VMEM),
        scratch_shapes=tile_scratch(settings, size),
        compiler_params=pltpu.CompilerParams(vmem_limit_bytes=VMEM_LIMIT),
        cost_estimate=pl.CostEstimate(flops=40_000_000_000, bytes_accessed=6_000_000, transcendentals=0),
    )(inverse, points, direction)


def cross_kernel(size, probes, inverse_ref, index_ref, first_ref, points_ref, direction_ref, far_ref,
                 ahead_ref, behind_ref, dist_ref, high_ref, low_ref):
    item = pl.program_id(0)
    features = points_ref.shape[0]
    at = pl.ds(pl.multiple_of(index_ref[item] * size, size), size)
    own = points_ref[:, at]
    far = far_ref[0, 0:features, :]
    anchor = jnp.where(first_ref[item] == 1, own[:, 0:1], far[:, 0:1])
    ahead, behind = tile_products(
        inverse_ref, own - anchor, far - anchor, direction_ref[:, at], far_ref[0, features:, :],
        dist_ref, high_ref, low_ref, probes
    )
    ahead_ref[0] = ahead
    behind_ref[0] = behind


def cross_products(inverse, index, first, points, direction, far, size):
    settings = inverse.shape[0]
    items, rows = far.shape[:2]
    columns = direction.shape[0]
    result = jax.ShapeDtypeStruct((items, columns, size), jnp.float32)
    result_spec = pl.BlockSpec((1, columns, size), lambda i: (i, 0, 0))
    return pl.pallas_call(
        functools.partial(cross_kernel, size, columns // settings),
        grid=(items,),
        out_shape=(result, result),
        in_specs=[pl.BlockSpec(memory_space=SMEM)] * 3
        + [pl.BlockSpec(memory_space=VMEM)] * 2
        + [pl.BlockSpec((1, rows, size), lambda i: (i, 0, 0))],
        out_specs=(result_spec, result_spec),
        scratch_shapes=tile_scratch(settings, size),
        compiler_params=pltpu.CompilerParams(vmem_limit_bytes=VMEM_LIMIT),
    )(inverse, index, first, points, direction, far)


def combine_kernel(size, probes, noise_ref, own_ref, own_live_ref, sent_ref, sent_live_ref, ahead_ref, arrived_ref,
                   diagonal_ref, direction_ref, residual_ref, image_ref, sums_ref):
    settings = noise_ref.shape[0]
    for setting in range(settings):
        rows = pl.ds(setting * probes, probes)
        image_ref[rows, :] = diagonal_ref[rows, :] + noise_ref[setting] * direction_ref[rows, :]

    def add(item, carry):
        @pl.when(own_live_ref[item] == 1)
        def _():
            at = pl.ds(pl.multiple_of(own_ref[item] * size, size), size)
            image_ref[:, at] += ahead_ref[item]

        @pl.when(sent_live_ref[item] == 1)
        def _():
            at = pl.ds(pl.multiple_of(sent_ref[item] * size, size), size)
            image_ref[:, at] += arrived_ref[item]

        return carry

    lax.fori_loop(0, ahead_ref.shape[0], add, 0)

    def total(chunk, sums):
        at = pl.ds(pl.multiple_of(chunk * 128, 128), 128)
        r, d, m = residual_ref[:, at], direction_ref[:, at], image_ref[:, at]
        return (sums[0] + r * r, sums[1] + d * m, sums[2] + r * m, sums[3] + m * m)

    zero = jnp.zeros((direction_ref.shape[0], 128), jnp.float32)
    sums = lax.fori_loop(0, direction_ref.shape[1] // 128, total, (zero,) * 4)
    for index in range(4):
        sums_ref[index] = sums[index]


def combine(noise, own, own_live, sent, sent_live, ahead, arrived, diagonal, direction, residual, size):
    columns = direction.shape[0]
    return pl.pallas_call(
        functools.partial(combine_kernel, size, columns // noise.shape[0]),
        out_shape=(
            jax.ShapeDtypeStruct(direction.shape, jnp.float32),
            jax.ShapeDtypeStruct((4, columns, 128), jnp.float32),
        ),
        in_specs=[pl.BlockSpec(memory_space=SMEM)] * 5 + [pl.BlockSpec(memory_space=VMEM)] * 5,
        out_specs=(pl.BlockSpec(memory_space=VMEM),) * 2,
        compiler_params=pltpu.CompilerParams(vmem_limit_bytes=VMEM_LIMIT),
    )(noise, own, own_live, sent, sent_live, ahead, arrived, diagonal, direction, residual)


def slot_tables(link_peer, my_index, devices):
    blocks = link_peer.shape[1]
    rounds = min(blocks, devices // 2 - 1)
    slots = (blocks + rounds - 1) // rounds
    halves = (slots + 1) // 2
    peers = jnp.arange(devices, dtype=jnp.int32)
    match = (link_peer[0, :rounds, 0][None, :] == peers[:, None]) | (link_peer[0, :rounds, 1][None, :] == peers[:, None])
    linked = jnp.any(match, axis=1)
    residue = jnp.sum(jnp.where(match, jnp.arange(rounds, dtype=jnp.int32)[None, :], 0), axis=1)
    first = (my_index < peers) == ((my_index + peers) % 2 == 0)
    half = jnp.arange(halves, dtype=jnp.int32)[None, :]

    def table(offset):
        slot = 2 * half + offset[:, None]
        block = residue[:, None] + rounds * slot
        live = linked[:, None] & (block < blocks)
        return jnp.where(live, block, 0).reshape(-1), live.astype(jnp.int32).reshape(-1)

    own, own_live = table(jnp.where(first, 0, 1))
    sent, sent_live = table(jnp.where(first, 1, 0))
    lower = jnp.repeat((my_index < peers).astype(jnp.int32), halves)
    return own, own_live, sent, sent_live, lower


def on_device(points, solution, residual, direction, lengthscales, noise_variance, link_peer):
    devices = lax.axis_size("wide")
    my_index = lax.axis_index("wide")
    size = points.shape[1] // link_peer.shape[1]
    probes = direction.shape[0] // lengthscales.shape[0]
    inverse = SCALE / lengthscales
    own, own_live, sent, sent_live, lower = slot_tables(link_peer, my_index, devices)
    outgoing = gather_blocks(sent, points, direction, size)
    incoming = lax.all_to_all(outgoing, "wide", split_axis=0, concat_axis=0, tiled=True)
    diagonal = diagonal_products(inverse, points, direction, size)
    ahead, behind = cross_products(inverse, own, lower, points, direction, incoming, size)
    arrived = lax.all_to_all(behind, "wide", split_axis=0, concat_axis=0, tiled=True)
    image, sums = combine(
        noise_variance, own, own_live, sent, sent_live, ahead, arrived, diagonal, direction, residual, size
    )
    totals = lax.psum(jnp.sum(sums, axis=2), "wide")
    old_norm, curvature, mixed, square = totals[0], totals[1], totals[2], totals[3]
    step_size = old_norm / curvature
    new_norm = old_norm - 2.0 * step_size * mixed + step_size * step_size * square
    ratio = new_norm / old_norm
    new_residual = residual - step_size[:, None] * image
    new_solution = solution + step_size[:, None] * direction
    new_direction = new_residual + ratio[:, None] * direction
    return (new_solution, new_residual, new_direction)


def solution(mesh):
    split = P(None, ("groups", "wide"))
    in_specs = (split, split, split, split, P(), P(), P(("groups", "wide"), None, None))
    return jax.shard_map(
        on_device, mesh=mesh, in_specs=in_specs, out_specs=(split,) * 3, check_vma=False
    )
```

```python
import functools

import jax
import jax.numpy as jnp
from jax import lax
from jax.experimental import pallas as pl
from jax.experimental.pallas import tpu as pltpu
from jax.sharding import PartitionSpec as P

VMEM = pltpu.VMEM
SMEM = pltpu.SMEM
MESH = pl.DeviceIdType.MESH
VMEM_LIMIT = 56 * 1024 * 1024
SCALE = 35.0 ** (1.0 / 36.0)
TOP = 36.0 * SCALE / 35.0
ROW_CHUNK = 32


def split_three(x):
    first = x.astype(jnp.bfloat16)
    rest = x - first.astype(jnp.float32)
    second = rest.astype(jnp.bfloat16)
    third = (rest - second.astype(jnp.float32)).astype(jnp.bfloat16)
    return first, second, third


def norm_rows(norms, low):
    pieces = [piece.astype(jnp.float32) for piece in split_three(norms)]
    row = lax.broadcasted_iota(jnp.int32, (16, norms.shape[1]), 0)
    rows = jnp.where((row >= 3 - low) & (row < 6 - low), 1.0, 0.0)
    for index, piece in enumerate(pieces):
        rows = jnp.where(row == index + low, piece, rows)
    return rows.astype(jnp.bfloat16)


def squared_distances(row_shift, col_shift):
    row_norms = jnp.sum(row_shift * row_shift, axis=0, keepdims=True)
    col_norms = jnp.sum(col_shift * col_shift, axis=0, keepdims=True)
    r1, r2, r3 = split_three(row_shift)
    c1, c2, c3 = split_three(-2.0 * col_shift)
    left = jnp.concatenate([r1, r1, r2, r1, r3, r2, norm_rows(row_norms, 0)], axis=0)
    right = jnp.concatenate([c1, c2, c1, c3, c1, c2, norm_rows(col_norms, 3)], axis=0)
    return lax.dot_general(
        left, right, (((0,), (0,)), ((), ())), preferred_element_type=jnp.float32
    )


def split_vectors(vectors, setting, probes):
    rows = vectors[setting * probes : (setting + 1) * probes]
    high = rows.astype(jnp.bfloat16).astype(jnp.float32)
    return jnp.concatenate([high, rows - high], axis=0).astype(jnp.bfloat16)


def apply_tile(vectors, high, low, dim):
    dims = (((1,), (dim,)), ((), ()))
    both = lax.dot_general(vectors, high, dims, preferred_element_type=jnp.float32)
    both += lax.dot_general(vectors, low, dims, preferred_element_type=jnp.float32)
    half = both.shape[0] // 2
    return both[:half] + both[half:]


def tile_products(inverse_ref, row_shift, col_shift, row_vectors, col_vectors, dist_ref, high_ref, low_ref, probes):
    size = row_shift.shape[1]
    settings = high_ref.shape[0]
    floor = jnp.maximum(squared_distances(row_shift, col_shift), 1e-30)
    dist_ref[...] = floor * lax.rsqrt(floor)
    ahead, behind = [], []
    for setting in range(settings):
        inverse = inverse_ref[setting]
        for start in range(0, size, ROW_CHUNK):
            rows = pl.ds(start, ROW_CHUNK)
            w = jnp.maximum(SCALE - dist_ref[rows, :] * inverse, 0.0)
            w2 = w * w
            w4 = w2 * w2
            w8 = w4 * w4
            w16 = w8 * w8
            w32 = w16 * w16
            value = (w32 * (w2 * w)) * (TOP - w)
            high = value.astype(jnp.bfloat16)
            high_ref[setting, rows, :] = high
            low_ref[setting, rows, :] = (value - high.astype(jnp.float32)).astype(jnp.bfloat16)
        high, low = high_ref[setting], low_ref[setting]
        behind.append(apply_tile(split_vectors(row_vectors, setting, probes), high, low, 0))
        if col_vectors is not None:
            ahead.append(apply_tile(split_vectors(col_vectors, setting, probes), high, low, 1))
    behind = jnp.concatenate(behind, axis=0)
    return (jnp.concatenate(ahead, axis=0) if ahead else None), behind


def gather_kernel(size, sent_ref, own_ref, points_ref, direction_ref, out_ref, kept_ref):
    features = points_ref.shape[0]

    def copy(item, carry):
        for index_ref, result_ref in ((sent_ref, out_ref), (own_ref, kept_ref)):
            block = pl.ds(pl.multiple_of(index_ref[item] * size, size), size)
            result_ref[item, 0:features, :] = points_ref[:, block]
            result_ref[item, features:, :] = direction_ref[:, block]
        return carry

    lax.fori_loop(0, out_ref.shape[0], copy, 0)


def gather_blocks(sent, own, points, direction, size):
    rows = points.shape[0] + direction.shape[0]
    return pl.pallas_call(
        functools.partial(gather_kernel, size),
        out_shape=(jax.ShapeDtypeStruct((sent.shape[0], rows, size), jnp.float32),) * 2,
        in_specs=[pl.BlockSpec(memory_space=SMEM)] * 2 + [pl.BlockSpec(memory_space=VMEM)] * 2,
        out_specs=(pl.BlockSpec(memory_space=VMEM),) * 2,
        compiler_params=pltpu.CompilerParams(vmem_limit_bytes=VMEM_LIMIT),
    )(sent, own, points, direction)


def greet(devices, me):
    barrier = pltpu.get_barrier_semaphore()

    def signal(step, carry):
        pl.semaphore_signal(barrier, inc=1, device_id={"wide": (me + step) % devices}, device_id_type=MESH)
        return carry

    lax.fori_loop(1, devices, signal, 0)
    pl.semaphore_wait(barrier, devices - 1)


def exchange_kernel(devices, slots, size, probes, inverse_ref, points_ref, direction_ref, kept_ref, outgoing_ref,
                    diagonal_ref, ahead_ref, arrived_ref, incoming_ref, behind_ref, dist_ref, high_ref, low_ref,
                    out_sems, in_sems, back_out_sems, back_in_sems):
    me = lax.axis_index("wide")
    halves = (slots + 1) // 2
    features = points_ref.shape[0]

    def shift(step):
        return devices // 2 + (step // 2) * (1 - 2 * (step % 2))

    def computed(peer):
        first = ((me < peer).astype(jnp.int32) + (me + peer) % 2) % 2
        return slots // 2 + first * (halves - slots // 2)

    def forward(peer, half):
        return pltpu.make_async_remote_copy(
            src_ref=outgoing_ref.at[peer * halves + half], dst_ref=incoming_ref.at[me * halves + half],
            send_sem=out_sems.at[peer * halves + half], recv_sem=in_sems.at[me * halves + half],
            device_id={"wide": peer}, device_id_type=MESH)

    def forward_arrival(peer, half):
        return pltpu.make_async_remote_copy(
            src_ref=outgoing_ref.at[peer * halves + half], dst_ref=incoming_ref.at[peer * halves + half],
            send_sem=out_sems.at[peer * halves + half], recv_sem=in_sems.at[peer * halves + half],
            device_id={"wide": peer}, device_id_type=MESH)

    def back(peer, half):
        return pltpu.make_async_remote_copy(
            src_ref=behind_ref.at[peer * halves + half], dst_ref=arrived_ref.at[me * halves + half],
            send_sem=back_out_sems.at[peer * halves + half], recv_sem=back_in_sems.at[me * halves + half],
            device_id={"wide": peer}, device_id_type=MESH)

    def back_arrival(peer, half):
        return pltpu.make_async_remote_copy(
            src_ref=behind_ref.at[peer * halves + half], dst_ref=arrived_ref.at[peer * halves + half],
            send_sem=back_out_sems.at[peer * halves + half], recv_sem=back_in_sems.at[peer * halves + half],
            device_id={"wide": peer}, device_id_type=MESH)

    def every(count_of, peer_of, action):
        def visit(step, carry):
            peer = peer_of(step)

            def one(half, inner):
                action(peer, half)
                return inner

            return lax.fori_loop(0, count_of(peer), one, carry)

        lax.fori_loop(1, devices, visit, 0)

    def target(step):
        return (me + shift(step)) % devices

    def source(step):
        return (me + devices - shift(step)) % devices

    greet(devices, me)
    every(lambda peer: slots - computed(peer), target, lambda peer, half: forward(peer, half).start())

    def diagonal_turn(block, carry):
        at = pl.ds(pl.multiple_of(block * size, size), size)
        own = points_ref[:, at]
        own = own - own[:, 0:1]
        _, product = tile_products(
            inverse_ref, own, own, direction_ref[:, at], None, dist_ref, high_ref, low_ref, probes
        )
        diagonal_ref[:, at] = product
        return carry

    lax.fori_loop(0, points_ref.shape[1] // size, diagonal_turn, 0)

    def cross_turn(peer, half):
        item = peer * halves + half
        forward_arrival(peer, half).wait_recv()
        own = kept_ref[item, 0:features, :]
        far = incoming_ref[item, 0:features, :]
        weight = (me < peer).astype(jnp.float32)
        anchor = weight * own[:, 0:1] + (1.0 - weight) * far[:, 0:1]
        ahead, behind = tile_products(
            inverse_ref, own - anchor, far - anchor, kept_ref[item, features:, :], incoming_ref[item, features:, :],
            dist_ref, high_ref, low_ref, probes
        )
        ahead_ref[item] = ahead
        behind_ref[item] = behind
        back(peer, half).start()

    every(computed, source, cross_turn)
    every(lambda peer: slots - computed(peer), target, lambda peer, half: forward(peer, half).wait_send())
    every(computed, source, lambda peer, half: back(peer, half).wait_send())
    every(lambda peer: slots - computed(peer), target, lambda peer, half: back_arrival(peer, half).wait_recv())


def tile_scratch(settings, size):
    return [
        pltpu.VMEM((size, size), jnp.float32),
        pltpu.VMEM((settings, size, size), jnp.bfloat16),
        pltpu.VMEM((settings, size, size), jnp.bfloat16),
    ]


def exchange_products(devices, slots, inverse, points, direction, kept, outgoing, size):
    settings = inverse.shape[0]
    items, rows = outgoing.shape[:2]
    columns = direction.shape[0]
    result = jax.ShapeDtypeStruct((items, columns, size), jnp.float32)
    return pl.pallas_call(
        functools.partial(exchange_kernel, devices, slots, size, columns // settings),
        out_shape=(jax.ShapeDtypeStruct(direction.shape, jnp.float32), result, result),
        in_specs=[pl.BlockSpec(memory_space=SMEM)]
        + [pl.BlockSpec(memory_space=VMEM)] * 3
        + [pl.BlockSpec(memory_space=pl.ANY)],
        out_specs=(pl.BlockSpec(memory_space=VMEM),) * 3,
        scratch_shapes=[pltpu.VMEM((items, rows, size), jnp.float32), pltpu.VMEM((items, columns, size), jnp.float32)]
        + tile_scratch(settings, size)
        + [pltpu.SemaphoreType.DMA((items,))] * 4,
        compiler_params=pltpu.CompilerParams(
            vmem_limit_bytes=VMEM_LIMIT, collective_id=0, has_side_effects=True
        ),
    )(inverse, points, direction, kept, outgoing)


def totals_kernel(devices, sums_ref, out_ref, held_ref, out_sems, in_sems):
    me = lax.axis_index("wide")
    greet(devices, me)

    def copy(target, slot):
        return pltpu.make_async_remote_copy(
            src_ref=sums_ref, dst_ref=held_ref.at[slot], send_sem=out_sems.at[target], recv_sem=in_sems.at[slot],
            device_id={"wide": target}, device_id_type=MESH)

    def send(step, carry):
        copy((me + step) % devices, me).start()
        return carry

    lax.fori_loop(1, devices, send, 0)
    held_ref[me] = sums_ref[...]

    def arrive(step, carry):
        peer = (me + step) % devices
        copy(peer, peer).wait()
        return carry

    lax.fori_loop(1, devices, arrive, 0)
    out_ref[...] = lax.fori_loop(
        1, devices, lambda peer, total: total + held_ref[peer], held_ref[0]
    )


def sum_over_devices(devices, sums):
    return pl.pallas_call(
        functools.partial(totals_kernel, devices),
        out_shape=jax.ShapeDtypeStruct(sums.shape, jnp.float32),
        in_specs=[pl.BlockSpec(memory_space=VMEM)],
        out_specs=pl.BlockSpec(memory_space=VMEM),
        scratch_shapes=[pltpu.VMEM((devices,) + sums.shape, jnp.float32)]
        + [pltpu.SemaphoreType.DMA((devices,))] * 2,
        compiler_params=pltpu.CompilerParams(collective_id=1, has_side_effects=True),
    )(sums)


def combine_kernel(size, probes, noise_ref, own_ref, own_live_ref, sent_ref, sent_live_ref, ahead_ref, arrived_ref,
                   diagonal_ref, direction_ref, residual_ref, image_ref, sums_ref):
    settings = noise_ref.shape[0]
    for setting in range(settings):
        rows = pl.ds(setting * probes, probes)
        image_ref[rows, :] = diagonal_ref[rows, :] + noise_ref[setting] * direction_ref[rows, :]

    def add(item, carry):
        @pl.when(own_live_ref[item] == 1)
        def _():
            at = pl.ds(pl.multiple_of(own_ref[item] * size, size), size)
            image_ref[:, at] += ahead_ref[item]

        @pl.when(sent_live_ref[item] == 1)
        def _():
            at = pl.ds(pl.multiple_of(sent_ref[item] * size, size), size)
            image_ref[:, at] += arrived_ref[item]

        return carry

    lax.fori_loop(0, ahead_ref.shape[0], add, 0)

    def total(chunk, sums):
        at = pl.ds(pl.multiple_of(chunk * 128, 128), 128)
        r, d, m = residual_ref[:, at], direction_ref[:, at], image_ref[:, at]
        return (sums[0] + r * r, sums[1] + d * m, sums[2] + r * m, sums[3] + m * m)

    zero = jnp.zeros((direction_ref.shape[0], 128), jnp.float32)
    sums = lax.fori_loop(0, direction_ref.shape[1] // 128, total, (zero,) * 4)
    lane = lax.broadcasted_iota(jnp.int32, zero.shape, 1)
    packed = zero
    for index in range(4):
        packed = jnp.where(lane == index, jnp.sum(sums[index], axis=1, keepdims=True), packed)
    sums_ref[...] = packed


def combine(noise, own, own_live, sent, sent_live, ahead, arrived, diagonal, direction, residual, size):
    columns = direction.shape[0]
    return pl.pallas_call(
        functools.partial(combine_kernel, size, columns // noise.shape[0]),
        out_shape=(
            jax.ShapeDtypeStruct(direction.shape, jnp.float32),
            jax.ShapeDtypeStruct((columns, 128), jnp.float32),
        ),
        in_specs=[pl.BlockSpec(memory_space=SMEM)] * 5 + [pl.BlockSpec(memory_space=VMEM)] * 5,
        out_specs=(pl.BlockSpec(memory_space=VMEM),) * 2,
        compiler_params=pltpu.CompilerParams(vmem_limit_bytes=VMEM_LIMIT),
    )(noise, own, own_live, sent, sent_live, ahead, arrived, diagonal, direction, residual)


def slot_tables(link_peer, my_index, devices):
    blocks = link_peer.shape[1]
    rounds = min(blocks, devices // 2 - 1)
    slots = (blocks + rounds - 1) // rounds
    halves = (slots + 1) // 2
    peers = jnp.arange(devices, dtype=jnp.int32)
    match = (link_peer[0, :rounds, 0][None, :] == peers[:, None]) | (link_peer[0, :rounds, 1][None, :] == peers[:, None])
    linked = jnp.any(match, axis=1)
    residue = jnp.sum(jnp.where(match, jnp.arange(rounds, dtype=jnp.int32)[None, :], 0), axis=1)
    first = (my_index < peers) == ((my_index + peers) % 2 == 0)
    half = jnp.arange(halves, dtype=jnp.int32)[None, :]

    def table(offset):
        slot = 2 * half + offset[:, None]
        block = residue[:, None] + rounds * slot
        live = linked[:, None] & (block < blocks)
        return jnp.where(live, block, 0).reshape(-1), live.astype(jnp.int32).reshape(-1)

    own, own_live = table(jnp.where(first, 0, 1))
    sent, sent_live = table(jnp.where(first, 1, 0))
    return slots, own, own_live, sent, sent_live


def on_device(points, solution, residual, direction, lengthscales, noise_variance, link_peer):
    devices = lax.axis_size("wide")
    my_index = lax.axis_index("wide")
    size = points.shape[1] // link_peer.shape[1]
    probes = direction.shape[0] // lengthscales.shape[0]
    inverse = SCALE / lengthscales
    slots, own, own_live, sent, sent_live = slot_tables(link_peer, my_index, devices)
    outgoing, kept = gather_blocks(sent, own, points, direction, size)
    diagonal, ahead, arrived = exchange_products(devices, slots, inverse, points, direction, kept, outgoing, size)
    image, sums = combine(
        noise_variance, own, own_live, sent, sent_live, ahead, arrived, diagonal, direction, residual, size
    )
    totals = sum_over_devices(devices, sums)
    old_norm, curvature, mixed, square = totals[:, 0], totals[:, 1], totals[:, 2], totals[:, 3]
    step_size = old_norm / curvature
    new_norm = old_norm - 2.0 * step_size * mixed + step_size * step_size * square
    ratio = new_norm / old_norm
    new_residual = residual - step_size[:, None] * image
    new_solution = solution + step_size[:, None] * direction
    new_direction = new_residual + ratio[:, None] * direction
    return (new_solution, new_residual, new_direction)


def solution(mesh):
    split = P(None, ("groups", "wide"))
    in_specs = (split, split, split, split, P(), P(), P(("groups", "wide"), None, None))
    return jax.shard_map(
        on_device, mesh=mesh, in_specs=in_specs, out_specs=(split,) * 3, check_vma=False
    )
```

```python
import functools

import jax
import jax.numpy as jnp
from jax import lax
from jax.experimental import pallas as pl
from jax.experimental.pallas import tpu as pltpu
from jax.sharding import PartitionSpec as P

VMEM = pltpu.VMEM
SMEM = pltpu.SMEM
MESH = pl.DeviceIdType.MESH
VMEM_LIMIT = 56 * 1024 * 1024
SCALE = 35.0 ** (1.0 / 36.0)
TOP = 36.0 * SCALE / 35.0
ROW_CHUNK = 32


def split_three(x):
    first = x.astype(jnp.bfloat16)
    rest = x - first.astype(jnp.float32)
    second = rest.astype(jnp.bfloat16)
    third = (rest - second.astype(jnp.float32)).astype(jnp.bfloat16)
    return first, second, third


def norm_rows(norms, low):
    pieces = [piece.astype(jnp.float32) for piece in split_three(norms)]
    row = lax.broadcasted_iota(jnp.int32, (16, norms.shape[1]), 0)
    rows = jnp.where((row >= 3 - low) & (row < 6 - low), 1.0, 0.0)
    for index, piece in enumerate(pieces):
        rows = jnp.where(row == index + low, piece, rows)
    return rows.astype(jnp.bfloat16)


def squared_distances(row_shift, col_shift):
    row_norms = jnp.sum(row_shift * row_shift, axis=0, keepdims=True)
    col_norms = jnp.sum(col_shift * col_shift, axis=0, keepdims=True)
    r1, r2, r3 = split_three(row_shift)
    c1, c2, c3 = split_three(-2.0 * col_shift)
    left = jnp.concatenate([r1, r1, r2, r1, r3, r2, norm_rows(row_norms, 0)], axis=0)
    right = jnp.concatenate([c1, c2, c1, c3, c1, c2, norm_rows(col_norms, 3)], axis=0)
    return lax.dot_general(
        left, right, (((0,), (0,)), ((), ())), preferred_element_type=jnp.float32
    )


def split_vectors(vectors, setting, probes):
    rows = vectors[setting * probes : (setting + 1) * probes]
    high = rows.astype(jnp.bfloat16).astype(jnp.float32)
    return jnp.concatenate([high, rows - high], axis=0).astype(jnp.bfloat16)


def apply_tile(vectors, high, low, dim):
    dims = (((1,), (dim,)), ((), ()))
    both = lax.dot_general(vectors, high, dims, preferred_element_type=jnp.float32)
    both += lax.dot_general(vectors, low, dims, preferred_element_type=jnp.float32)
    half = both.shape[0] // 2
    return both[:half] + both[half:]


def tile_products(inverse_ref, row_shift, col_shift, row_vectors, col_vectors, dist_ref, high_ref, low_ref, probes):
    size = row_shift.shape[1]
    settings = high_ref.shape[0]
    floor = jnp.maximum(squared_distances(row_shift, col_shift), 1e-30)
    dist_ref[...] = floor * lax.rsqrt(floor)
    ahead, behind = [], []
    for setting in range(settings):
        inverse = inverse_ref[setting]
        for start in range(0, size, ROW_CHUNK):
            rows = pl.ds(start, ROW_CHUNK)
            w = jnp.maximum(SCALE - dist_ref[rows, :] * inverse, 0.0)
            w2 = w * w
            w4 = w2 * w2
            w8 = w4 * w4
            w16 = w8 * w8
            w32 = w16 * w16
            value = (w32 * (w2 * w)) * (TOP - w)
            high = value.astype(jnp.bfloat16)
            high_ref[setting, rows, :] = high
            low_ref[setting, rows, :] = (value - high.astype(jnp.float32)).astype(jnp.bfloat16)
        high, low = high_ref[setting], low_ref[setting]
        behind.append(apply_tile(split_vectors(row_vectors, setting, probes), high, low, 0))
        if col_vectors is not None:
            ahead.append(apply_tile(split_vectors(col_vectors, setting, probes), high, low, 1))
    behind = jnp.concatenate(behind, axis=0)
    return (jnp.concatenate(ahead, axis=0) if ahead else None), behind


def gather_kernel(size, sent_ref, own_ref, points_ref, direction_ref, out_ref, kept_ref):
    features = points_ref.shape[0]

    base = pl.program_id(0) * out_ref.shape[0]

    def copy(item, carry):
        for index_ref, result_ref in ((sent_ref, out_ref), (own_ref, kept_ref)):
            block = pl.ds(pl.multiple_of(index_ref[base + item] * size, size), size)
            result_ref[item, 0:features, :] = points_ref[:, block]
            result_ref[item, features:, :] = direction_ref[:, block]
        return carry

    lax.fori_loop(0, out_ref.shape[0], copy, 0)


def gather_blocks(sent, own, points, direction, size):
    rows = points.shape[0] + direction.shape[0]
    items = sent.shape[0]
    group = 8 if items % 8 == 0 else 1
    result_spec = pl.BlockSpec((group, rows, size), lambda i: (i, 0, 0))
    return pl.pallas_call(
        functools.partial(gather_kernel, size),
        grid=(items // group,),
        out_shape=(jax.ShapeDtypeStruct((sent.shape[0], rows, size), jnp.float32),) * 2,
        in_specs=[pl.BlockSpec(memory_space=SMEM)] * 2 + [pl.BlockSpec(memory_space=VMEM)] * 2,
        out_specs=(result_spec,) * 2,
        compiler_params=pltpu.CompilerParams(vmem_limit_bytes=VMEM_LIMIT),
    )(sent, own, points, direction)


def greet(devices, me):
    barrier = pltpu.get_barrier_semaphore()

    def signal(step, carry):
        pl.semaphore_signal(barrier, inc=1, device_id={"wide": (me + step) % devices}, device_id_type=MESH)
        return carry

    lax.fori_loop(1, devices, signal, 0)
    pl.semaphore_wait(barrier, devices - 1)


def exchange_kernel(devices, slots, size, probes, inverse_ref, points_hbm, direction_hbm, kept_hbm, outgoing_ref,
                    diagonal_ref, ahead_ref, arrived_ref, incoming_ref, behind_ref, dist_ref, high_ref, low_ref,
                    points_ref, direction_ref, kept_ref, local_sems, out_sems, in_sems, back_out_sems, back_in_sems):
    me = lax.axis_index("wide")
    halves = (slots + 1) // 2
    features = points_ref.shape[0]

    def shift(step):
        return (step * (devices // 2 - 1)) % devices

    def computed(peer):
        first = ((me < peer).astype(jnp.int32) + (me + peer) % 2) % 2
        return slots // 2 + first * (halves - slots // 2)

    def forward(peer, half):
        return pltpu.make_async_remote_copy(
            src_ref=outgoing_ref.at[peer * halves + half], dst_ref=incoming_ref.at[me * halves + half],
            send_sem=out_sems.at[peer * halves + half], recv_sem=in_sems.at[me * halves + half],
            device_id={"wide": peer}, device_id_type=MESH)

    def forward_arrival(peer, half):
        return pltpu.make_async_remote_copy(
            src_ref=outgoing_ref.at[peer * halves + half], dst_ref=incoming_ref.at[peer * halves + half],
            send_sem=out_sems.at[peer * halves + half], recv_sem=in_sems.at[peer * halves + half],
            device_id={"wide": peer}, device_id_type=MESH)

    def back(peer, half):
        return pltpu.make_async_remote_copy(
            src_ref=behind_ref.at[peer * halves + half], dst_ref=arrived_ref.at[me * halves + half],
            send_sem=back_out_sems.at[peer * halves + half], recv_sem=back_in_sems.at[me * halves + half],
            device_id={"wide": peer}, device_id_type=MESH)

    def back_arrival(peer, half):
        return pltpu.make_async_remote_copy(
            src_ref=behind_ref.at[peer * halves + half], dst_ref=arrived_ref.at[peer * halves + half],
            send_sem=back_out_sems.at[peer * halves + half], recv_sem=back_in_sems.at[peer * halves + half],
            device_id={"wide": peer}, device_id_type=MESH)

    def every(count_of, peer_of, action):
        def visit(step, carry):
            peer = peer_of(step)

            def one(half, inner):
                action(peer, half)
                return inner

            return lax.fori_loop(0, count_of(peer), one, carry)

        lax.fori_loop(1, devices, visit, 0)

    def target(step):
        return (me + shift(step)) % devices

    def source(step):
        return (me + devices - shift(step)) % devices

    greet(devices, me)
    every(lambda peer: slots - computed(peer), target, lambda peer, half: forward(peer, half).start())
    points_copy = pltpu.make_async_copy(points_hbm, points_ref, local_sems.at[0])
    direction_copy = pltpu.make_async_copy(direction_hbm, direction_ref, local_sems.at[1])
    kept_copy = pltpu.make_async_copy(kept_hbm, kept_ref, local_sems.at[2])
    points_copy.start()
    direction_copy.start()
    kept_copy.start()
    points_copy.wait()
    direction_copy.wait()

    def diagonal_turn(block, carry):
        at = pl.ds(pl.multiple_of(block * size, size), size)
        own = points_ref[:, at]
        own = own - own[:, 0:1]
        _, product = tile_products(
            inverse_ref, own, own, direction_ref[:, at], None, dist_ref, high_ref, low_ref, probes
        )
        diagonal_ref[:, at] = product
        return carry

    lax.fori_loop(0, points_ref.shape[1] // size, diagonal_turn, 0)
    kept_copy.wait()

    def cross_turn(peer, half):
        item = peer * halves + half
        forward_arrival(peer, half).wait_recv()
        own = kept_ref[item, 0:features, :]
        far = incoming_ref[item, 0:features, :]
        weight = (me < peer).astype(jnp.float32)
        anchor = weight * own[:, 0:1] + (1.0 - weight) * far[:, 0:1]
        ahead, behind = tile_products(
            inverse_ref, own - anchor, far - anchor, kept_ref[item, features:, :], incoming_ref[item, features:, :],
            dist_ref, high_ref, low_ref, probes
        )
        ahead_ref[item] = ahead
        behind_ref[item] = behind
        back(peer, half).start()

    every(computed, source, cross_turn)
    every(lambda peer: slots - computed(peer), target, lambda peer, half: forward(peer, half).wait_send())
    every(computed, source, lambda peer, half: back(peer, half).wait_send())
    every(lambda peer: slots - computed(peer), target, lambda peer, half: back_arrival(peer, half).wait_recv())


def tile_scratch(settings, size):
    return [
        pltpu.VMEM((size, size), jnp.float32),
        pltpu.VMEM((settings, size, size), jnp.bfloat16),
        pltpu.VMEM((settings, size, size), jnp.bfloat16),
    ]


def exchange_products(devices, slots, inverse, points, direction, kept, outgoing, size):
    settings = inverse.shape[0]
    items, rows = outgoing.shape[:2]
    columns = direction.shape[0]
    result = jax.ShapeDtypeStruct((items, columns, size), jnp.float32)
    return pl.pallas_call(
        functools.partial(exchange_kernel, devices, slots, size, columns // settings),
        out_shape=(jax.ShapeDtypeStruct(direction.shape, jnp.float32), result, result),
        in_specs=[pl.BlockSpec(memory_space=SMEM)] + [pl.BlockSpec(memory_space=pl.ANY)] * 4,
        out_specs=(pl.BlockSpec(memory_space=VMEM),) * 3,
        scratch_shapes=[pltpu.VMEM((items, rows, size), jnp.float32), pltpu.VMEM((items, columns, size), jnp.float32)]
        + tile_scratch(settings, size)
        + [pltpu.VMEM(array.shape, jnp.float32) for array in (points, direction, kept)]
        + [pltpu.SemaphoreType.DMA((3,))]
        + [pltpu.SemaphoreType.DMA((items,))] * 4,
        compiler_params=pltpu.CompilerParams(
            vmem_limit_bytes=VMEM_LIMIT, collective_id=0, has_side_effects=True
        ),
    )(inverse, points, direction, kept, outgoing)


def totals_kernel(devices, sums_ref, out_ref, held_ref, out_sems, in_sems):
    me = lax.axis_index("wide")
    greet(devices, me)

    def copy(target, slot):
        return pltpu.make_async_remote_copy(
            src_ref=sums_ref, dst_ref=held_ref.at[slot], send_sem=out_sems.at[target], recv_sem=in_sems.at[slot],
            device_id={"wide": target}, device_id_type=MESH)

    def send(step, carry):
        copy((me + step) % devices, me).start()
        return carry

    lax.fori_loop(1, devices, send, 0)
    held_ref[me] = sums_ref[...]

    def arrive(step, carry):
        peer = (me + step) % devices
        copy(peer, peer).wait()
        return carry

    lax.fori_loop(1, devices, arrive, 0)
    out_ref[...] = lax.fori_loop(
        1, devices, lambda peer, total: total + held_ref[peer], held_ref[0]
    )


def sum_over_devices(devices, sums):
    return pl.pallas_call(
        functools.partial(totals_kernel, devices),
        out_shape=jax.ShapeDtypeStruct(sums.shape, jnp.float32),
        in_specs=[pl.BlockSpec(memory_space=VMEM)],
        out_specs=pl.BlockSpec(memory_space=VMEM),
        scratch_shapes=[pltpu.VMEM((devices,) + sums.shape, jnp.float32)]
        + [pltpu.SemaphoreType.DMA((devices,))] * 2,
        compiler_params=pltpu.CompilerParams(collective_id=1, has_side_effects=True),
    )(sums)


def combine_kernel(size, probes, noise_ref, own_ref, own_live_ref, sent_ref, sent_live_ref, ahead_ref, arrived_ref,
                   diagonal_ref, direction_ref, residual_ref, image_ref, sums_ref):
    settings = noise_ref.shape[0]
    for setting in range(settings):
        rows = pl.ds(setting * probes, probes)
        image_ref[rows, :] = diagonal_ref[rows, :] + noise_ref[setting] * direction_ref[rows, :]

    def add(item, carry):
        @pl.when(own_live_ref[item] == 1)
        def _():
            at = pl.ds(pl.multiple_of(own_ref[item] * size, size), size)
            image_ref[:, at] += ahead_ref[item]

        @pl.when(sent_live_ref[item] == 1)
        def _():
            at = pl.ds(pl.multiple_of(sent_ref[item] * size, size), size)
            image_ref[:, at] += arrived_ref[item]

        return carry

    lax.fori_loop(0, ahead_ref.shape[0], add, 0)

    def total(chunk, sums):
        at = pl.ds(pl.multiple_of(chunk * 128, 128), 128)
        r, d, m = residual_ref[:, at], direction_ref[:, at], image_ref[:, at]
        return (sums[0] + r * r, sums[1] + d * m, sums[2] + r * m, sums[3] + m * m)

    zero = jnp.zeros((direction_ref.shape[0], 128), jnp.float32)
    sums = lax.fori_loop(0, direction_ref.shape[1] // 128, total, (zero,) * 4)
    lane = lax.broadcasted_iota(jnp.int32, zero.shape, 1)
    packed = zero
    for index in range(4):
        packed = jnp.where(lane == index, jnp.sum(sums[index], axis=1, keepdims=True), packed)
    sums_ref[...] = packed


def combine(noise, own, own_live, sent, sent_live, ahead, arrived, diagonal, direction, residual, size):
    columns = direction.shape[0]
    return pl.pallas_call(
        functools.partial(combine_kernel, size, columns // noise.shape[0]),
        out_shape=(
            jax.ShapeDtypeStruct(direction.shape, jnp.float32),
            jax.ShapeDtypeStruct((columns, 128), jnp.float32),
        ),
        in_specs=[pl.BlockSpec(memory_space=SMEM)] * 5 + [pl.BlockSpec(memory_space=VMEM)] * 5,
        out_specs=(pl.BlockSpec(memory_space=VMEM),) * 2,
        compiler_params=pltpu.CompilerParams(vmem_limit_bytes=VMEM_LIMIT),
    )(noise, own, own_live, sent, sent_live, ahead, arrived, diagonal, direction, residual)


def slot_tables(link_peer, my_index, devices):
    blocks = link_peer.shape[1]
    rounds = min(blocks, devices // 2 - 1)
    slots = (blocks + rounds - 1) // rounds
    halves = (slots + 1) // 2
    peers = jnp.arange(devices, dtype=jnp.int32)
    match = (link_peer[0, :rounds, 0][None, :] == peers[:, None]) | (link_peer[0, :rounds, 1][None, :] == peers[:, None])
    linked = jnp.any(match, axis=1)
    residue = jnp.sum(jnp.where(match, jnp.arange(rounds, dtype=jnp.int32)[None, :], 0), axis=1)
    first = (my_index < peers) == ((my_index + peers) % 2 == 0)
    half = jnp.arange(halves, dtype=jnp.int32)[None, :]

    def table(offset):
        slot = 2 * half + offset[:, None]
        block = residue[:, None] + rounds * slot
        live = linked[:, None] & (block < blocks)
        return jnp.where(live, block, 0).reshape(-1), live.astype(jnp.int32).reshape(-1)

    own, own_live = table(jnp.where(first, 0, 1))
    sent, sent_live = table(jnp.where(first, 1, 0))
    return slots, own, own_live, sent, sent_live


def on_device(points, solution, residual, direction, lengthscales, noise_variance, link_peer):
    devices = lax.axis_size("wide")
    my_index = lax.axis_index("wide")
    size = points.shape[1] // link_peer.shape[1]
    probes = direction.shape[0] // lengthscales.shape[0]
    inverse = SCALE / lengthscales
    slots, own, own_live, sent, sent_live = slot_tables(link_peer, my_index, devices)
    outgoing, kept = gather_blocks(sent, own, points, direction, size)
    diagonal, ahead, arrived = exchange_products(devices, slots, inverse, points, direction, kept, outgoing, size)
    image, sums = combine(
        noise_variance, own, own_live, sent, sent_live, ahead, arrived, diagonal, direction, residual, size
    )
    totals = sum_over_devices(devices, sums)
    old_norm, curvature, mixed, square = totals[:, 0], totals[:, 1], totals[:, 2], totals[:, 3]
    step_size = old_norm / curvature
    new_norm = old_norm - 2.0 * step_size * mixed + step_size * step_size * square
    ratio = new_norm / old_norm
    new_residual = residual - step_size[:, None] * image
    new_solution = solution + step_size[:, None] * direction
    new_direction = new_residual + ratio[:, None] * direction
    return (new_solution, new_residual, new_direction)


def solution(mesh):
    split = P(None, ("groups", "wide"))
    in_specs = (split, split, split, split, P(), P(), P(("groups", "wide"), None, None))
    return jax.shard_map(
        on_device, mesh=mesh, in_specs=in_specs, out_specs=(split,) * 3, check_vma=False
    )
```

```python
import functools

import jax
import jax.numpy as jnp
from jax import lax
from jax.experimental import pallas as pl
from jax.experimental.pallas import tpu as pltpu
from jax.sharding import PartitionSpec as P

VMEM = pltpu.VMEM
SMEM = pltpu.SMEM
MESH = pl.DeviceIdType.MESH
VMEM_LIMIT = 56 * 1024 * 1024
SCALE = 35.0 ** (1.0 / 36.0)
TOP = 36.0 * SCALE / 35.0
ROW_CHUNK = 32


def split_three(x):
    first = x.astype(jnp.bfloat16)
    rest = x - first.astype(jnp.float32)
    second = rest.astype(jnp.bfloat16)
    third = (rest - second.astype(jnp.float32)).astype(jnp.bfloat16)
    return first, second, third


def norm_rows(norms, low):
    pieces = [piece.astype(jnp.float32) for piece in split_three(norms)]
    row = lax.broadcasted_iota(jnp.int32, (16, norms.shape[1]), 0)
    rows = jnp.where((row >= 3 - low) & (row < 6 - low), 1.0, 0.0)
    for index, piece in enumerate(pieces):
        rows = jnp.where(row == index + low, piece, rows)
    return rows.astype(jnp.bfloat16)


def squared_distances(row_shift, col_shift):
    row_norms = jnp.sum(row_shift * row_shift, axis=0, keepdims=True)
    col_norms = jnp.sum(col_shift * col_shift, axis=0, keepdims=True)
    r1, r2, r3 = split_three(row_shift)
    c1, c2, c3 = split_three(-2.0 * col_shift)
    left = jnp.concatenate([r1, r1, r2, r1, r3, r2, norm_rows(row_norms, 0)], axis=0)
    right = jnp.concatenate([c1, c2, c1, c3, c1, c2, norm_rows(col_norms, 3)], axis=0)
    return lax.dot_general(
        left, right, (((0,), (0,)), ((), ())), preferred_element_type=jnp.float32
    )


def split_vectors(vectors, setting, probes):
    rows = vectors[setting * probes : (setting + 1) * probes]
    high = rows.astype(jnp.bfloat16).astype(jnp.float32)
    return jnp.concatenate([high, rows - high], axis=0).astype(jnp.bfloat16)


def apply_tile(vectors, high, low, dim):
    dims = (((1,), (dim,)), ((), ()))
    both = lax.dot_general(vectors, high, dims, preferred_element_type=jnp.float32)
    both += lax.dot_general(vectors, low, dims, preferred_element_type=jnp.float32)
    half = both.shape[0] // 2
    return both[:half] + both[half:]


def tile_products(inverse_ref, row_shift, col_shift, row_vectors, col_vectors, dist_ref, high_ref, low_ref, probes):
    size = row_shift.shape[1]
    settings = high_ref.shape[0]
    floor = jnp.maximum(squared_distances(row_shift, col_shift), 1e-30)
    dist_ref[...] = floor * lax.rsqrt(floor)
    ahead, behind = [], []
    for setting in range(settings):
        inverse = inverse_ref[setting]
        for start in range(0, size, ROW_CHUNK):
            rows = pl.ds(start, ROW_CHUNK)
            w = jnp.maximum(SCALE - dist_ref[rows, :] * inverse, 0.0)
            w2 = w * w
            w4 = w2 * w2
            w8 = w4 * w4
            w16 = w8 * w8
            w32 = w16 * w16
            value = (w32 * (w2 * w)) * (TOP - w)
            high = value.astype(jnp.bfloat16)
            high_ref[setting, rows, :] = high
            low_ref[setting, rows, :] = (value - high.astype(jnp.float32)).astype(jnp.bfloat16)
        high, low = high_ref[setting], low_ref[setting]
        behind.append(apply_tile(split_vectors(row_vectors, setting, probes), high, low, 0))
        if col_vectors is not None:
            ahead.append(apply_tile(split_vectors(col_vectors, setting, probes), high, low, 1))
    behind = jnp.concatenate(behind, axis=0)
    return (jnp.concatenate(ahead, axis=0) if ahead else None), behind


def gather_kernel(size, sent_ref, own_ref, points_ref, direction_ref, out_ref, kept_ref):
    features = points_ref.shape[0]

    base = pl.program_id(0) * out_ref.shape[0]

    def copy(item, carry):
        for index_ref, result_ref in ((sent_ref, out_ref), (own_ref, kept_ref)):
            block = pl.ds(pl.multiple_of(index_ref[base + item] * size, size), size)
            result_ref[item, 0:features, :] = points_ref[:, block]
            result_ref[item, features:, :] = direction_ref[:, block]
        return carry

    lax.fori_loop(0, out_ref.shape[0], copy, 0)


def gather_blocks(sent, own, points, direction, size):
    rows = points.shape[0] + direction.shape[0]
    items = sent.shape[0]
    group = 8 if items % 8 == 0 else 1
    result_spec = pl.BlockSpec((group, rows, size), lambda i: (i, 0, 0))
    return pl.pallas_call(
        functools.partial(gather_kernel, size),
        grid=(items // group,),
        out_shape=(jax.ShapeDtypeStruct((sent.shape[0], rows, size), jnp.float32),) * 2,
        in_specs=[pl.BlockSpec(memory_space=SMEM)] * 2 + [pl.BlockSpec(memory_space=VMEM)] * 2,
        out_specs=(result_spec,) * 2,
        compiler_params=pltpu.CompilerParams(vmem_limit_bytes=VMEM_LIMIT),
    )(sent, own, points, direction)


def greet(devices, me):
    barrier = pltpu.get_barrier_semaphore()

    def signal(step, carry):
        pl.semaphore_signal(barrier, inc=1, device_id={"wide": (me + step) % devices}, device_id_type=MESH)
        return carry

    lax.fori_loop(1, devices, signal, 0)
    pl.semaphore_wait(barrier, devices - 1)


def exchange_kernel(devices, slots, size, probes, inverse_ref, points_hbm, direction_hbm, kept_hbm, outgoing_ref,
                    diagonal_ref, ahead_ref, arrived_ref, incoming_ref, behind_ref, dist_ref, high_ref, low_ref,
                    points_ref, direction_ref, kept_ref, local_sems, out_sems, in_sems, back_out_sems, back_in_sems):
    me = lax.axis_index("wide")
    halves = (slots + 1) // 2
    features = points_ref.shape[0]

    def shift(step):
        return (step * (devices // 2 - 1)) % devices

    def computed(peer):
        first = ((me < peer).astype(jnp.int32) + (me + peer) % 2) % 2
        return slots // 2 + first * (halves - slots // 2)

    def forward(peer, half):
        return pltpu.make_async_remote_copy(
            src_ref=outgoing_ref.at[peer * halves + half], dst_ref=incoming_ref.at[me * halves + half],
            send_sem=out_sems.at[peer * halves + half], recv_sem=in_sems.at[me * halves + half],
            device_id={"wide": peer}, device_id_type=MESH)

    def forward_arrival(peer, half):
        return pltpu.make_async_remote_copy(
            src_ref=outgoing_ref.at[peer * halves + half], dst_ref=incoming_ref.at[peer * halves + half],
            send_sem=out_sems.at[peer * halves + half], recv_sem=in_sems.at[peer * halves + half],
            device_id={"wide": peer}, device_id_type=MESH)

    def back(peer, half):
        return pltpu.make_async_remote_copy(
            src_ref=behind_ref.at[peer * halves + half], dst_ref=arrived_ref.at[me * halves + half],
            send_sem=back_out_sems.at[peer * halves + half], recv_sem=back_in_sems.at[me * halves + half],
            device_id={"wide": peer}, device_id_type=MESH)

    def back_arrival(peer, half):
        return pltpu.make_async_remote_copy(
            src_ref=behind_ref.at[peer * halves + half], dst_ref=arrived_ref.at[peer * halves + half],
            send_sem=back_out_sems.at[peer * halves + half], recv_sem=back_in_sems.at[peer * halves + half],
            device_id={"wide": peer}, device_id_type=MESH)

    def every(count_of, peer_of, action):
        def visit(step, carry):
            peer = peer_of(step)

            def one(half, inner):
                action(peer, half)
                return inner

            return lax.fori_loop(0, count_of(peer), one, carry)

        lax.fori_loop(1, devices, visit, 0)

    def target(step):
        return (me + shift(step)) % devices

    def source(step):
        return (me + devices - shift(step)) % devices

    greet(devices, me)
    every(lambda peer: slots - computed(peer), target, lambda peer, half: forward(peer, half).start())
    points_copy = pltpu.make_async_copy(points_hbm, points_ref, local_sems.at[0])
    direction_copy = pltpu.make_async_copy(direction_hbm, direction_ref, local_sems.at[1])
    kept_copy = pltpu.make_async_copy(kept_hbm, kept_ref, local_sems.at[2])
    points_copy.start()
    direction_copy.start()
    kept_copy.start()
    points_copy.wait()
    direction_copy.wait()

    def diagonal_turn(block, carry):
        at = pl.ds(pl.multiple_of(block * size, size), size)
        own = points_ref[:, at]
        own = own - own[:, 0:1]
        _, product = tile_products(
            inverse_ref, own, own, direction_ref[:, at], None, dist_ref, high_ref, low_ref, probes
        )
        diagonal_ref[:, at] = product
        return carry

    lax.fori_loop(0, points_ref.shape[1] // size, diagonal_turn, 0)
    kept_copy.wait()

    def cross_turn(peer, half):
        item = peer * halves + half
        forward_arrival(peer, half).wait_recv()
        own = kept_ref[item, 0:features, :]
        far = incoming_ref[item, 0:features, :]
        weight = (me < peer).astype(jnp.float32)
        anchor = weight * own[:, 0:1] + (1.0 - weight) * far[:, 0:1]
        ahead, behind = tile_products(
            inverse_ref, own - anchor, far - anchor, kept_ref[item, features:, :], incoming_ref[item, features:, :],
            dist_ref, high_ref, low_ref, probes
        )
        ahead_ref[item] = ahead
        behind_ref[item] = behind
        back(peer, half).start()

    every(computed, source, cross_turn)
    every(lambda peer: slots - computed(peer), target, lambda peer, half: forward(peer, half).wait_send())
    every(computed, source, lambda peer, half: back(peer, half).wait_send())
    every(lambda peer: slots - computed(peer), target, lambda peer, half: back_arrival(peer, half).wait_recv())


def tile_scratch(settings, size):
    return [
        pltpu.VMEM((size, size), jnp.float32),
        pltpu.VMEM((settings, size, size), jnp.bfloat16),
        pltpu.VMEM((settings, size, size), jnp.bfloat16),
    ]


def exchange_products(devices, slots, inverse, points, direction, kept, outgoing, size):
    settings = inverse.shape[0]
    items, rows = outgoing.shape[:2]
    columns = direction.shape[0]
    result = jax.ShapeDtypeStruct((items, columns, size), jnp.float32)
    return pl.pallas_call(
        functools.partial(exchange_kernel, devices, slots, size, columns // settings),
        out_shape=(jax.ShapeDtypeStruct(direction.shape, jnp.float32), result, result),
        in_specs=[pl.BlockSpec(memory_space=SMEM)] + [pl.BlockSpec(memory_space=pl.ANY)] * 4,
        out_specs=(pl.BlockSpec(memory_space=VMEM),) * 3,
        scratch_shapes=[pltpu.VMEM((items, rows, size), jnp.float32), pltpu.VMEM((items, columns, size), jnp.float32)]
        + tile_scratch(settings, size)
        + [pltpu.VMEM(array.shape, jnp.float32) for array in (points, direction, kept)]
        + [pltpu.SemaphoreType.DMA((3,))]
        + [pltpu.SemaphoreType.DMA((items,))] * 4,
        compiler_params=pltpu.CompilerParams(
            vmem_limit_bytes=VMEM_LIMIT, collective_id=0, has_side_effects=True
        ),
    )(inverse, points, direction, kept, outgoing)


def totals_kernel(devices, sums_ref, out_ref, held_ref, out_sems, in_sems):
    me = lax.axis_index("wide")
    greet(devices, me)

    def copy(target, slot):
        return pltpu.make_async_remote_copy(
            src_ref=sums_ref, dst_ref=held_ref.at[slot], send_sem=out_sems.at[target], recv_sem=in_sems.at[slot],
            device_id={"wide": target}, device_id_type=MESH)

    def send(step, carry):
        copy((me + step) % devices, me).start()
        return carry

    lax.fori_loop(1, devices, send, 0)
    held_ref[me] = sums_ref[...]

    def arrive(step, carry):
        peer = (me + step) % devices
        copy(peer, peer).wait()
        return carry

    lax.fori_loop(1, devices, arrive, 0)
    out_ref[...] = lax.fori_loop(
        1, devices, lambda peer, total: total + held_ref[peer], held_ref[0]
    )


def sum_over_devices(devices, sums):
    return pl.pallas_call(
        functools.partial(totals_kernel, devices),
        out_shape=jax.ShapeDtypeStruct(sums.shape, jnp.float32),
        in_specs=[pl.BlockSpec(memory_space=VMEM)],
        out_specs=pl.BlockSpec(memory_space=VMEM),
        scratch_shapes=[pltpu.VMEM((devices,) + sums.shape, jnp.float32)]
        + [pltpu.SemaphoreType.DMA((devices,))] * 2,
        compiler_params=pltpu.CompilerParams(collective_id=1, has_side_effects=True),
    )(sums)


def combine_kernel(size, probes, noise_ref, own_ref, own_live_ref, sent_ref, sent_live_ref, ahead_hbm, arrived_hbm,
                   residual_hbm, diagonal_ref, direction_ref, image_ref, sums_ref, ahead_ref, arrived_ref,
                   residual_ref, sems):
    pairs = ((ahead_hbm, ahead_ref), (arrived_hbm, arrived_ref), (residual_hbm, residual_ref))
    copies = [pltpu.make_async_copy(pair[0], pair[1], sems.at[i]) for i, pair in enumerate(pairs)]
    for copy in copies:
        copy.start()
    settings = noise_ref.shape[0]
    for setting in range(settings):
        rows = pl.ds(setting * probes, probes)
        image_ref[rows, :] = diagonal_ref[rows, :] + noise_ref[setting] * direction_ref[rows, :]

    copies[0].wait()
    copies[1].wait()

    def add(item, carry):
        @pl.when(own_live_ref[item] == 1)
        def _():
            at = pl.ds(pl.multiple_of(own_ref[item] * size, size), size)
            image_ref[:, at] += ahead_ref[item]

        @pl.when(sent_live_ref[item] == 1)
        def _():
            at = pl.ds(pl.multiple_of(sent_ref[item] * size, size), size)
            image_ref[:, at] += arrived_ref[item]

        return carry

    lax.fori_loop(0, ahead_ref.shape[0], add, 0)
    copies[2].wait()

    def total(chunk, sums):
        at = pl.ds(pl.multiple_of(chunk * 128, 128), 128)
        r, d, m = residual_ref[:, at], direction_ref[:, at], image_ref[:, at]
        return (sums[0] + r * r, sums[1] + d * m, sums[2] + r * m, sums[3] + m * m)

    zero = jnp.zeros((direction_ref.shape[0], 128), jnp.float32)
    sums = lax.fori_loop(0, direction_ref.shape[1] // 128, total, (zero,) * 4, unroll=2)
    lane = lax.broadcasted_iota(jnp.int32, zero.shape, 1)
    packed = zero
    for index in range(4):
        packed = jnp.where(lane == index, jnp.sum(sums[index], axis=1, keepdims=True), packed)
    sums_ref[...] = packed


def combine(noise, own, own_live, sent, sent_live, ahead, arrived, diagonal, direction, residual, size):
    columns = direction.shape[0]
    return pl.pallas_call(
        functools.partial(combine_kernel, size, columns // noise.shape[0]),
        out_shape=(
            jax.ShapeDtypeStruct(direction.shape, jnp.float32),
            jax.ShapeDtypeStruct((columns, 128), jnp.float32),
        ),
        in_specs=[pl.BlockSpec(memory_space=SMEM)] * 5
        + [pl.BlockSpec(memory_space=pl.ANY)] * 3
        + [pl.BlockSpec(memory_space=VMEM)] * 2,
        out_specs=(pl.BlockSpec(memory_space=VMEM),) * 2,
        scratch_shapes=[pltpu.VMEM(array.shape, jnp.float32) for array in (ahead, arrived, residual)]
        + [pltpu.SemaphoreType.DMA((3,))],
        compiler_params=pltpu.CompilerParams(vmem_limit_bytes=VMEM_LIMIT),
    )(noise, own, own_live, sent, sent_live, ahead, arrived, residual, diagonal, direction)


def slot_tables(link_peer, my_index, devices):
    blocks = link_peer.shape[1]
    rounds = min(blocks, devices // 2 - 1)
    slots = (blocks + rounds - 1) // rounds
    halves = (slots + 1) // 2
    peers = jnp.arange(devices, dtype=jnp.int32)
    match = (link_peer[0, :rounds, 0][None, :] == peers[:, None]) | (link_peer[0, :rounds, 1][None, :] == peers[:, None])
    linked = jnp.any(match, axis=1)
    residue = jnp.sum(jnp.where(match, jnp.arange(rounds, dtype=jnp.int32)[None, :], 0), axis=1)
    first = (my_index < peers) == ((my_index + peers) % 2 == 0)
    half = jnp.arange(halves, dtype=jnp.int32)[None, :]

    def table(offset):
        slot = 2 * half + offset[:, None]
        block = residue[:, None] + rounds * slot
        live = linked[:, None] & (block < blocks)
        return jnp.where(live, block, 0).reshape(-1), live.astype(jnp.int32).reshape(-1)

    own, own_live = table(jnp.where(first, 0, 1))
    sent, sent_live = table(jnp.where(first, 1, 0))
    return slots, own, own_live, sent, sent_live


def on_device(points, solution, residual, direction, lengthscales, noise_variance, link_peer):
    devices = lax.axis_size("wide")
    my_index = lax.axis_index("wide")
    size = points.shape[1] // link_peer.shape[1]
    probes = direction.shape[0] // lengthscales.shape[0]
    inverse = SCALE / lengthscales
    slots, own, own_live, sent, sent_live = slot_tables(link_peer, my_index, devices)
    outgoing, kept = gather_blocks(sent, own, points, direction, size)
    diagonal, ahead, arrived = exchange_products(devices, slots, inverse, points, direction, kept, outgoing, size)
    image, sums = combine(
        noise_variance, own, own_live, sent, sent_live, ahead, arrived, diagonal, direction, residual, size
    )
    totals = sum_over_devices(devices, sums)
    old_norm, curvature, mixed, square = totals[:, 0], totals[:, 1], totals[:, 2], totals[:, 3]
    step_size = old_norm / curvature
    new_norm = old_norm - 2.0 * step_size * mixed + step_size * step_size * square
    ratio = new_norm / old_norm
    new_residual = residual - step_size[:, None] * image
    new_solution = solution + step_size[:, None] * direction
    new_direction = new_residual + ratio[:, None] * direction
    return (new_solution, new_residual, new_direction)


def solution(mesh):
    split = P(None, ("groups", "wide"))
    in_specs = (split, split, split, split, P(), P(), P(("groups", "wide"), None, None))
    return jax.shard_map(
        on_device, mesh=mesh, in_specs=in_specs, out_specs=(split,) * 3, check_vma=False
    )
```
